512 devices in a mesh: rows: 32 (over x, y), tp: 16 (over z, core).
Axes of the slice: x: 4, y: 8, z: 8, core: 2. Of those that a mesh axis runs over, the one named last changes fastest.
Arguments:
- queries: bfloat16 [8192, 8192], P('rows', 'tp'), may hold values from -32 to 32
- nbr_keys: bfloat16 [32768, 8192], P(('rows', 'tp')), may hold values from -8 to 8
- nbr_values: bfloat16 [32768, 8192], P(('rows', 'tp')), may hold values from -15 to 15
- nbr_index: int32 [128, 2], P('rows'), may hold values from 0 to 7, all different within a row
- residual: bfloat16 [8192, 8192], P(('rows', 'tp')), may hold values from -2 to 2
- out_weight: bfloat16 [8192, 8192], P('tp', 'rows'), may hold values from -0.0625 to 0.0625
Outputs:
- mixed: bfloat16 [8192, 8192], P(('rows', 'tp'))
The draws below stay inside these ranges and needn't reach their ends.
Inputs may be any that keep to these rules, and one draw needn't show every extreme that they name: `nbr_index`: the 2 entries of a span differ; they index the 8 neighbours retrieved for that span's own sequence shard.
All inputs are finite; a program needn't handle non-finite values.
Results may differ from the reference program's by a relative error of at most 0.022.
Values may be sent and summed in bfloat16 or wider, within the bound.
A program may use at most 64 MiB of HBM per device.

```python
import math
import jax
import jax.numpy as jnp
from jax import lax

D = 8192
H = 64
HD = 128
CH = 64
R = 128
KN = 2
TOK_DEV = 256
NBG = 8
HEADS_DEV = 4
TOKENS = 8192
SPANS = 128
NBROWS = 32768
N_ROWS = 32


def draw_queries(key, part):
    key = jax.random.fold_in(key, 11)
    background = jax.random.normal(key, (TOKENS, H * HD), jnp.float32)
    return jnp.clip(background, -6.0, 6.0).astype(jnp.bfloat16)


def draw_nbr_keys(key, part):
    key = jax.random.fold_in(key, 23)
    first_key = jax.random.fold_in(key, 0)
    background = jax.random.normal(first_key, (NBROWS, H * HD), jnp.float32)
    return jnp.clip(background, -6.0, 6.0).astype(jnp.bfloat16)


def levels(rng, extent, cuts, low, largest):
    loudness, own = 1.0, jax.random.fold_in(rng, 6)
    for position, blocks in cuts:
        draws = jnp.exp(jax.random.uniform(jax.random.fold_in(own, position), (blocks,), jnp.float32, low / len(cuts), largest / len(cuts)))
        loudness = loudness * jnp.repeat(draws, extent[position] // blocks).reshape([-1 if axis == position else 1 for axis in range(len(extent))])
    return loudness


def choose_distinct(rng, rows, count, top, lift):
    ranking = jax.random.permutation(jax.random.fold_in(rng, 1), count)
    boost = ranking
    for power in range(3):
        boost = boost * boost // count
    boost = boost * lift // count
    tickets = jax.random.randint(jax.random.fold_in(rng, 2), (rows, count), 0, 4096) + boost
    holders = jax.random.permutation(jax.random.fold_in(rng, 3), rows)[jnp.arange(count) % rows]
    tickets = jnp.where(jnp.arange(rows)[:, None] == holders[None, :], 1 << 14, tickets)
    priority = tickets * count + jnp.arange(count)
    return lax.top_k(priority.astype(jnp.int32), top)[1].astype(jnp.int32)


def scatter_about(stream_key, extent, spread, most, cuts=(), kind=jnp.bfloat16):
    array = jax.random.normal(stream_key, extent, jnp.float32) * spread
    if len(cuts) > 0:
        array = levels(stream_key, extent, cuts, -0.22, 0.18) * array
    return jnp.clip(array, min=-most, max=most).astype(kind)


def setup_inputs(seed: int = 0) -> dict:
    splits = jax.random.split(jax.random.key(seed), 7)
    queries = draw_queries(jax.random.fold_in(splits[6], 71), 0)
    nbr_keys = draw_nbr_keys(jax.random.fold_in(splits[6], 71), 0)
    nbr_values = scatter_about(splits[2], (NBROWS, H * HD), 3.0, 15.0, ((0, 512),))
    nbr_index = choose_distinct(splits[3], SPANS, NBG, KN, 4096)
    residual = scatter_about(splits[4], (TOKENS, D), 0.3, 2.0, ((0, 512),))
    out_weight = scatter_about(splits[5], (H * HD, D), (H * HD) ** -0.5, 0.0625, ((0, 16), (1, 32)))
    return {"queries": queries, "nbr_keys": nbr_keys, "nbr_values": nbr_values, "nbr_index": nbr_index, "residual": residual, "out_weight": out_weight}


def reference(queries, nbr_keys, nbr_values, nbr_index, residual, out_weight):
    span_dev = TOK_DEV // CH
    score_scale = 1.0 / math.sqrt(HD)
    query_blocks = queries.reshape(N_ROWS, span_dev, CH, H, HD)
    key_blocks = nbr_keys.reshape(N_ROWS, NBG, R, H, HD)
    value_blocks = nbr_values.reshape(N_ROWS, NBG, R, H, HD)
    chosen_rows = nbr_index.reshape(N_ROWS, span_dev, KN)

    def shard_attend(pieces):
        shard_queries, shard_keys, shard_values, chosen = pieces
        picked_keys = shard_keys[chosen]
        picked_values = shard_values[chosen]
        scores = jnp.einsum('cqhd,ckrhd->chqkr', shard_queries.astype(jnp.float32), picked_keys.astype(jnp.float32)) * score_scale
        row_top = lax.optimization_barrier(jnp.max(scores, axis=(3, 4), keepdims=True))
        weights = jnp.exp(scores - row_top)
        probs = (weights / lax.optimization_barrier(jnp.sum(weights, axis=(3, 4), keepdims=True))).astype(jnp.bfloat16)
        attended = jnp.einsum('chqkr,ckrhd->cqhd', probs.astype(jnp.float32), picked_values.astype(jnp.float32))
        return attended.astype(jnp.bfloat16)
    attn = lax.map(shard_attend, (query_blocks, key_blocks, value_blocks, chosen_rows)).reshape(TOKENS, H * HD)
    group_width = HEADS_DEV * HD
    accumulated = residual.astype(jnp.float32)
    for head_group in range(H // HEADS_DEV):
        columns = attn[:, head_group * group_width:(head_group + 1) * group_width]
        partial_value = jnp.dot(columns, out_weight[head_group * group_width:(head_group + 1) * group_width], preferred_element_type=jnp.float32)
        accumulated = accumulated + lax.optimization_barrier(partial_value.astype(jnp.bfloat16)).astype(jnp.float32)
    return accumulated.astype(jnp.bfloat16)
```

```python
import functools
import heapq
import math

import jax
import jax.numpy as jnp
from jax import lax
from jax.experimental import pallas as pl
from jax.experimental.pallas import tpu as pltpu
from jax.sharding import PartitionSpec as P

MESH = pl.DeviceIdType.MESH
F32, BF16 = jnp.float32, jnp.bfloat16

HD, CH, R = 128, 64, 128
NX, NY, NZ = 4, 8, 8
TP, ROWS = 16, 32
TOK, HCOLS, WCOLS, KROWS = 256, 512, 256, 64
D = 8192
SPANS, HEADS = TOK // CH, HCOLS // HD
TOKZ, TOKD = TOK // NZ, TOK // TP
HALF = D // 2
G = 4
GC = HALF // G
GB = GC // WCOLS

PARTS = ((0, 208, 112), (208, 512, 352))


def gather_plan():
    messages, needs = [], []

    def add(part, axis, sign, dx, dy, piece, need):
        lo, hi, mid = PARTS[part]
        lo, hi = ((lo, hi), (lo, mid), (mid, hi))[piece]
        messages.append((axis, sign, dx, dy, lo, hi))
        needs.append(need)
        return len(messages) - 1

    def ring(part, axis, size, other, need):
        got = {0: need}
        for sign in (1, -1):
            for step in range(size // 2):
                at = -sign * step
                last = step == size // 2 - 1
                piece = 0 if not last else (1 if sign == 1 else 2)
                dx, dy = (at, other) if axis == 0 else (other, at)
                bring = add(part, axis, sign, dx, dy, piece, got[at])
                key = size // 2 if last else at - sign
                got[key] = got.get(key, ()) + (bring,) if last else (bring,)
        return got

    for bx, need in ring(0, 0, NX, 0, ()).items():
        ring(0, 1, NY, bx, need)
    for by, need in ring(1, 1, NY, 0, ()).items():
        ring(1, 0, NX, by, need)

    count = len(messages)
    feeds = [[j for j in range(count) if i in needs[j]] for i in range(count)]
    depth = [0] * count
    for i in reversed(range(count)):
        depth[i] = max([1 + depth[j] for j in feeds[i]], default=0)
    rate, delay = 2 * WCOLS * 2 / 90e3, 1.5
    free = {}
    queue = []
    left = [len(n) for n in needs]

    def launch(i, now):
        axis, sign, _, _, lo, hi = messages[i]
        begin = max(now, free.get((axis, sign), 0.0))
        free[axis, sign] = begin + (hi - lo) * rate
        heapq.heappush(queue, (free[axis, sign] + delay, i))

    first = sorted((i for i in range(count) if not needs[i]), key=lambda i: (-depth[i], i))
    for i in first:
        launch(i, 0.0)
    steps = []
    while queue:
        now, i = heapq.heappop(queue)
        ready = []
        for j in feeds[i]:
            left[j] -= 1
            if left[j] == 0:
                ready.append(j)
        ready.sort(key=lambda j: (-depth[j], j))
        for j in ready:
            launch(j, now)
        steps.append((now, i, ready, not feeds[i]))
    return messages, first, steps


MESSAGES, FIRST, STEPS = gather_plan()


def kernel(
    do_kv, do_w, do_rs, score_at,
    idx_ref, q_ref, k_ref, v_ref, res_ref, w_ref, out_ref,
    kbuf, vbuf, qbuf, rbuf, wbuf, attn, probs, xsend, xrecv, pown, sbuf, rplus, rminus, fin,
    local_sem, kv_send, kv_recv, w_send, w_recv, r_send, r_recv, x_send, x_recv, c_send, c_recv, f_send, f_recv,
):
    row, tp = lax.axis_index("rows"), lax.axis_index("tp")
    x, y = row // NY, row % NY
    z, core = tp // 2, tp % 2
    sibling = z * 2 + (1 - core)

    def at_z(dz, dc=0):
        return ((z + dz) % NZ) * 2 + (core + dc) % 2

    def at_xy(axis, sign):
        if axis == 0:
            return ((x + sign) % NX) * NY + y
        return x * NY + (y + sign) % NY

    partners = [(row, sibling)]
    partners += [(row, at_z(dz, dc)) for dz in (4, 3, -3, 2, -2, 1, -1) for dc in (0, 1)]
    around = [(at_xy(axis, sign), tp) for axis in (0, 1) for sign in (1, -1)]

    barrier = pltpu.get_barrier_semaphore()
    for who in partners + around:
        pl.semaphore_signal(barrier, inc=1, device_id=who, device_id_type=MESH)

    own = (z, pl.ds(pl.multiple_of(core * KROWS, KROWS), KROWS))
    own_cols = pl.multiple_of(tp * HCOLS, HCOLS)
    my_half = pl.multiple_of(core * HALF, HALF)
    its_half = pl.multiple_of((1 - core) * HALF, HALF)
    my_rows = pl.ds(pl.multiple_of(core * TOKD, TOKD), TOKD)
    its_rows = pl.ds(pl.multiple_of((1 - core) * TOKD, TOKD), TOKD)

    locals_ = [
        pltpu.make_async_copy(q_ref, qbuf, local_sem.at[0]),
        pltpu.make_async_copy(k_ref.at[:, pl.ds(own_cols, HCOLS)], kbuf.at[own], kv_recv.at[0]),
        pltpu.make_async_copy(v_ref.at[:, pl.ds(own_cols, HCOLS)], vbuf.at[own], kv_recv.at[1]),
        pltpu.make_async_copy(w_ref, wbuf.at[row], local_sem.at[3]),
        pltpu.make_async_copy(res_ref.at[:, pl.ds(my_half, HALF)], rbuf.at[my_rows], local_sem.at[4]),
    ]
    for copy in locals_:
        copy.start()
    pl.semaphore_wait(barrier, len(partners) + len(around))

    def owner(dx, dy):
        return ((x + dx) % NX) * NY + (y + dy) % NY

    def w_copy(i, arrived):
        axis, sign, dx, dy, lo, hi = MESSAGES[i]
        if arrived:
            dx, dy = (dx - sign, dy) if axis == 0 else (dx, dy - sign)
        slot = wbuf.at[owner(dx, dy), pl.ds(lo, hi - lo), :]
        mine = not arrived and dx == 0 and dy == 0
        return pltpu.make_async_remote_copy(
            src_ref=w_ref.at[pl.ds(lo, hi - lo), :] if mine else slot,
            dst_ref=slot,
            send_sem=w_send,
            recv_sem=w_recv.at[i],
            device_id=(at_xy(axis, sign), tp),
            device_id_type=MESH,
        )

    if do_w:
        for i in FIRST:
            w_copy(i, False).start()
    if do_kv:
        for which, (src, dst) in enumerate(((k_ref, kbuf), (v_ref, vbuf))):
            for _, to in partners[1:] + partners[:1]:
                pltpu.make_async_remote_copy(
                    src_ref=src.at[:, pl.ds(pl.multiple_of(to * HCOLS, HCOLS), HCOLS)],
                    dst_ref=dst.at[own],
                    send_sem=kv_send.at[which],
                    recv_sem=kv_recv.at[which],
                    device_id=(row, to),
                    device_id_type=MESH,
                ).start()
    residual_copy = pltpu.make_async_remote_copy(
        src_ref=res_ref.at[:, pl.ds(its_half, HALF)],
        dst_ref=rbuf.at[my_rows],
        send_sem=r_send,
        recv_sem=r_recv,
        device_id=(row, sibling),
        device_id_type=MESH,
    )
    residual_copy.start()

    def kv_wait(which):
        buf = (kbuf, vbuf)[which]
        if do_kv:
            pltpu.make_async_copy(buf, buf, kv_recv.at[which]).wait()
        else:
            locals_[1 + which].wait()

    def score(span):
        rows = pl.ds(span * CH, CH)
        keys = [kbuf[idx_ref[span, k]] for k in range(2)]
        for h in range(HEADS):
            query = qbuf[rows, h * HD:(h + 1) * HD]
            raw = jnp.concatenate(
                [
                    lax.dot_general(
                        query, block[:, h * HD:(h + 1) * HD], (((1,), (1,)), ((), ())),
                        preferred_element_type=F32,
                    )
                    for block in keys
                ],
                axis=1,
            ) * (1.0 / math.sqrt(HD))
            weights = jnp.exp(raw - jnp.max(raw, axis=1, keepdims=True))
            total = jnp.sum(weights, axis=1, keepdims=True)
            probs[rows, h * 2 * R:(h + 1) * 2 * R] = (weights / total).astype(BF16)

    def attend(span):
        rows = pl.ds(span * CH, CH)
        values = [vbuf[idx_ref[span, k]] for k in range(2)]
        for h in range(HEADS):
            value = jnp.concatenate([block[:, h * HD:(h + 1) * HD] for block in values], axis=0)
            out = jnp.dot(probs[rows, h * 2 * R:(h + 1) * 2 * R], value, preferred_element_type=F32)
            attn[rows, h * HD:(h + 1) * HD] = out.astype(BF16)

    locals_[0].wait()
    scored = False
    late = []
    if do_w:
        for now, i, sends, last in STEPS:
            if now > score_at and not scored:
                scored = True
                kv_wait(0)
                for span in range(SPANS):
                    score(span)
            if last:
                late.append(i)
                continue
            w_copy(i, True).wait_recv()
            for j in sends:
                w_copy(j, False).start()
    if not scored:
        kv_wait(0)
        for span in range(SPANS):
            score(span)
    kv_wait(1)
    for span in range(SPANS):
        attend(span)
    for i in late:
        w_copy(i, True).wait_recv()
    for copy in locals_[3:]:
        copy.wait()
    residual_copy.wait()

    def chain(g, step, sign):
        buf = rplus if sign == 1 else rminus
        way = 0 if sign == 1 else 1
        if step == 0:
            tokens = pl.ds(pl.multiple_of(((z + 4) % NZ) * TOKZ, TOKZ), TOKZ)
            cols = pl.ds(way * (GC // 2), GC // 2)
            src, dst = sbuf.at[g, tokens, cols], buf.at[g, 0, :, cols]
        else:
            src, dst = buf.at[g, step - 1], buf.at[g, step]
        return pltpu.make_async_remote_copy(
            src_ref=src,
            dst_ref=dst,
            send_sem=c_send.at[way, g, step],
            recv_sem=c_recv.at[way, g, step],
            device_id=(row, at_z(sign)),
            device_id_type=MESH,
        )

    def tokens_of(dz):
        return pl.ds(pl.multiple_of(((z + dz) % NZ) * TOKZ, TOKZ), TOKZ)

    def exchange(g):
        return pltpu.make_async_remote_copy(
            src_ref=xsend.at[g],
            dst_ref=xrecv.at[g],
            send_sem=x_send.at[g],
            recv_sem=x_recv.at[g],
            device_id=(row, sibling),
            device_id_type=MESH,
        )

    def project(g):
        for side in (1 - core, core):
            for j in range(GB):
                block = wbuf[side * (ROWS // 2) + g * GB + j]
                part = jnp.dot(attn[...], block, preferred_element_type=F32)
                cols = slice(j * WCOLS, (j + 1) * WCOLS)
                if side is core:
                    pown[g, :, cols] = part
                else:
                    xsend[g, :, cols] = part.astype(BF16)
            if side is not core:
                exchange(g).start()

    def combine(g):
        exchange(g).wait_recv()
        sbuf[g] = (pown[g] + xrecv[g].astype(F32)).astype(BF16)
        for sign in (1, -1):
            chain(g, 0, sign).start()

    def relay(g, step):
        for sign in (1, -1):
            buf = rplus if sign == 1 else rminus
            chain(g, step - 1, sign).wait_recv()
            tokens = tokens_of(sign * (4 - step))
            if step == 1:
                cut = GC // 2
                got, rest = (slice(0, cut), slice(cut, GC)) if sign == 1 else (slice(cut, GC), slice(0, cut))
                buf[g, 0, :, got] = (buf[g, 0, :, got].astype(F32) + sbuf[g, tokens, got].astype(F32)).astype(BF16)
                buf[g, 0, :, rest] = sbuf[g, tokens, rest]
            else:
                buf[g, step - 1] = (buf[g, step - 1].astype(F32) + sbuf[g, tokens, :].astype(F32)).astype(BF16)
            chain(g, step, sign).start()

    def final_copy(g, cols):
        return pltpu.make_async_remote_copy(
            src_ref=fin.at[g],
            dst_ref=out_ref.at[:, cols],
            send_sem=f_send.at[g],
            recv_sem=f_recv.at[g],
            device_id=(row, sibling),
            device_id_type=MESH,
        )

    def finish(g):
        for sign in (1, -1):
            chain(g, 3, sign).wait_recv()
        cols = pl.ds(g * GC, GC)
        for rows, base in ((its_rows, (1 - core) * TOKD), (my_rows, core * TOKD)):
            tokens = pl.ds(pl.multiple_of(z * TOKZ + base, TOKD), TOKD)
            total = (
                rbuf[rows, cols].astype(F32)
                + sbuf[g, tokens, :].astype(F32)
                + rplus[g, 3, rows, :].astype(F32)
                + rminus[g, 3, rows, :].astype(F32)
            ).astype(BF16)
            if rows is its_rows:
                fin[g] = total
                final_copy(g, pl.ds(pl.multiple_of(my_half + g * GC, GC), GC)).start()
            else:
                out_ref[:, pl.ds(pl.multiple_of(my_half + g * GC, GC), GC)] = total

    if do_rs:
        for wave in range(G + 5):
            if wave < G:
                project(wave)
            for step in range(5):
                g = wave - 1 - step
                if 0 <= g < G:
                    if step == 0:
                        combine(g)
                    elif step < 4:
                        relay(g, step)
                    else:
                        finish(g)
        for g in range(G):
            final_copy(g, pl.ds(pl.multiple_of(its_half + g * GC, GC), GC)).wait_recv()
        for g in range(G):
            exchange(g).wait_send()
            final_copy(g, pl.ds(pl.multiple_of(my_half + g * GC, GC), GC)).wait_send()
            for step in range(4):
                for sign in (1, -1):
                    chain(g, step, sign).wait_send()
    else:
        out_ref[...] = jnp.zeros_like(out_ref)
        out_ref[:, 0:HCOLS] = attn[0:TOKD, :]
    if do_kv:
        waitbuf = wbuf.at[pl.ds(0, TP - 1), pl.ds(0, KROWS * HCOLS // WCOLS), :]
        for which in range(2):
            pltpu.make_async_copy(waitbuf, waitbuf, kv_send.at[which]).wait()
    if do_w:
        rest = wbuf.at[pl.ds(0, ROWS - 1)]
        pltpu.make_async_copy(rest, rest, w_send).wait()


def build(mesh, do_kv=True, do_w=True, do_rs=True, score_at=30.0, collective_id=0):
    def shards(queries, nbr_keys, nbr_values, nbr_index, residual, out_weight):
        hbm = pl.BlockSpec(memory_space=pl.ANY)
        dma = pltpu.SemaphoreType.DMA
        return pl.pallas_call(
            functools.partial(kernel, do_kv, do_w, do_rs, score_at),
            out_shape=jax.ShapeDtypeStruct((TOKD, D), BF16),
            in_specs=[pl.BlockSpec(memory_space=pltpu.SMEM)] + [hbm] * 5,
            out_specs=pl.BlockSpec(memory_space=pltpu.VMEM),
            scratch_shapes=[
                pltpu.VMEM((NZ, R, HCOLS), BF16),
                pltpu.VMEM((NZ, R, HCOLS), BF16),
                pltpu.VMEM((TOK, HCOLS), BF16),
                pltpu.VMEM((TOKZ, HALF), BF16),
                pltpu.VMEM((ROWS, HCOLS, WCOLS), BF16),
                pltpu.VMEM((TOK, HCOLS), BF16),
                pltpu.VMEM((TOK, HEADS * 2 * R), BF16),
                pltpu.VMEM((G, TOK, GC), BF16),
                pltpu.VMEM((G, TOK, GC), BF16),
                pltpu.VMEM((G, TOK, GC), F32),
                pltpu.VMEM((G, TOK, GC), BF16),
                pltpu.VMEM((G, 4, TOKZ, GC), BF16),
                pltpu.VMEM((G, 4, TOKZ, GC), BF16),
                pltpu.VMEM((G, TOKD, GC), BF16),
                dma((5,)), dma((2,)), dma((2,)), dma, dma((len(MESSAGES),)), dma, dma,
                dma((G,)), dma((G,)), dma((2, G, 4)), dma((2, G, 4)), dma((G,)), dma((G,)),
            ],
            compiler_params=pltpu.CompilerParams(
                collective_id=collective_id, has_side_effects=True, vmem_limit_bytes=48 * 1024 * 1024
            ),
            cost_estimate=pl.CostEstimate(flops=2_400_000_000, bytes_accessed=12_000_000, transcendentals=262144),
        )(nbr_index, queries, nbr_keys, nbr_values, residual, out_weight)

    placed = (
        P("rows", "tp"),
        P(("rows", "tp"), None),
        P(("rows", "tp"), None),
        P("rows", None),
        P(("rows", "tp"), None),
        P("tp", "rows"),
    )
    return jax.shard_map(
        shards, mesh=mesh, in_specs=placed, out_specs=P(("rows", "tp"), None), check_vma=False
    )


def solution(mesh):
    return build(mesh)
```

```python
import heapq
import math

import jax
import jax.numpy as jnp
from jax import lax
from jax.experimental import pallas as pl
from jax.experimental.pallas import tpu as pltpu
from jax.sharding import PartitionSpec as P

MESH = pl.DeviceIdType.MESH
F32, BF16 = jnp.float32, jnp.bfloat16

HD, CH, R = 128, 64, 128
NX, NY, NZ = 4, 8, 8
TP, ROWS = 16, 32
TOK, HCOLS, WCOLS, KROWS = 256, 512, 256, 64
D = 8192
SPANS, HEADS = TOK // CH, HCOLS // HD
TOKZ, TOKD = TOK // NZ, TOK // TP
HALF = D // 2
G = 4
GC = HALF // G
GB = GC // WCOLS

PARTS = ((0, 208, 112), (208, 512, 352))

SCORE_AT = 30.0


def gather_plan():
    messages, needs = [], []

    def add(part, axis, sign, dx, dy, piece, need):
        lo, hi, mid = PARTS[part]
        lo, hi = ((lo, hi), (lo, mid), (mid, hi))[piece]
        messages.append((axis, sign, dx, dy, lo, hi))
        needs.append(need)
        return len(messages) - 1

    def ring(part, axis, size, other, need):
        got = {0: need}
        for sign in (1, -1):
            for step in range(size // 2):
                at = -sign * step
                last = step == size // 2 - 1
                piece = 0 if not last else (1 if sign == 1 else 2)
                dx, dy = (at, other) if axis == 0 else (other, at)
                bring = add(part, axis, sign, dx, dy, piece, got[at])
                key = size // 2 if last else at - sign
                got[key] = got.get(key, ()) + (bring,) if last else (bring,)
        return got

    for bx, need in ring(0, 0, NX, 0, ()).items():
        ring(0, 1, NY, bx, need)
    for by, need in ring(1, 1, NY, 0, ()).items():
        ring(1, 0, NX, by, need)

    count = len(messages)
    feeds = [[j for j in range(count) if i in needs[j]] for i in range(count)]
    depth = [0] * count
    for i in reversed(range(count)):
        depth[i] = max([1 + depth[j] for j in feeds[i]], default=0)
    rate, delay = 2 * WCOLS * 2 / 90e3, 1.5
    free = {}
    queue = []
    left = [len(n) for n in needs]

    def launch(i, now):
        axis, sign, _, _, lo, hi = messages[i]
        begin = max(now, free.get((axis, sign), 0.0))
        free[axis, sign] = begin + (hi - lo) * rate
        heapq.heappush(queue, (free[axis, sign] + delay, i))

    first = sorted((i for i in range(count) if not needs[i]), key=lambda i: (-depth[i], i))
    for i in first:
        launch(i, 0.0)
    steps = []
    while queue:
        now, i = heapq.heappop(queue)
        ready = []
        for j in feeds[i]:
            left[j] -= 1
            if left[j] == 0:
                ready.append(j)
        ready.sort(key=lambda j: (-depth[j], j))
        for j in ready:
            launch(j, now)
        steps.append((now, i, ready, not feeds[i]))
    return messages, first, steps


MESSAGES, FIRST, STEPS = gather_plan()


def wrap(axis, d):
    size = (NX, NY)[axis]
    return (d + size // 2 - 1) % size - (size // 2 - 1)


def came(i):
    axis, sign, dx, dy, _, _ = MESSAGES[i]
    return (wrap(0, dx - sign), wrap(1, dy)) if axis == 0 else (wrap(0, dx), wrap(1, dy - sign))


def arrival_order():
    when = {(0, 0): 0.0}
    for now, i, _, _ in STEPS:
        when[came(i)] = now
    return sorted(when, key=lambda at: (when[at], at))


ORDER = arrival_order()


def place(i):
    return ORDER.index(came(i))


def sum_plan():
    project_us, meet_us, small_us, link_us, delay_us = 7.0 / G, 1.6, 0.3, 6.0 / G, 1.6
    now, free = 0.0, 0.0
    ready = []
    order, left = [], list(range(G))
    while left or ready:
        able = sorted((-stage, g) for t, stage, g in ready if t <= now)
        if able:
            stage, g = -able[0][0], able[0][1]
            ready = [r for r in ready if r[1:] != (stage, g)]
            now += small_us
            order.append((1, g, 0) if stage == 0 else (2, g, stage) if stage < 4 else (3, g, 0))
            if stage < 4:
                free = max(now, free) + link_us * (0.5 if stage == 0 else 1.0)
                ready.append((free + delay_us, stage + 1, g))
        elif left:
            g = left.pop(0)
            order.append((0, g, 0))
            ready.append((now + project_us / 2 + meet_us, 0, g))
            now += project_us
        else:
            now = min(t for t, _, _ in ready)
    return order, now


SUMS, SUMS_US = sum_plan()


def kernel(
    idx_hbm, q_ref, k_ref, v_ref, res_ref, w_ref, out_ref,
    idx_ref, kbuf, vbuf, qbuf, rbuf, wbuf, attn, probs, xsend, xrecv, pown, sbuf, shared, chains, ends,
    idx_sem, local_sem, kv_send, kv_recv, w_send, w_recv,
    x_send, x_recv, s_send, s_recv, c_send, c_recv, e_send, e_recv,
):
    row, tp = lax.axis_index("rows"), lax.axis_index("tp")
    x, y = row // NY, row % NY
    z, core = tp // 2, tp % 2
    sibling = z * 2 + (1 - core)

    def at_z(dz, dc=0):
        return ((z + dz) % NZ) * 2 + (core + dc) % 2

    def at_xy(axis, sign):
        if axis == 0:
            return ((x + sign) % NX) * NY + y
        return x * NY + (y + sign) % NY

    partners = [(row, sibling)]
    partners += [(row, at_z(dz, dc)) for dz in (4, 3, -3, 2, -2, 1, -1) for dc in (0, 1)]
    around = [(at_xy(axis, sign), tp) for axis in (0, 1) for sign in (1, -1)]

    barrier = pltpu.get_barrier_semaphore()
    for who in partners + around:
        pl.semaphore_signal(barrier, inc=1, device_id=who, device_id_type=MESH)

    own = (z, pl.ds(pl.multiple_of(core * KROWS, KROWS), KROWS))
    own_cols = pl.multiple_of(tp * HCOLS, HCOLS)

    fetch = pltpu.make_async_copy(idx_hbm, idx_ref, idx_sem)
    fetch.start()
    locals_ = [
        pltpu.make_async_copy(q_ref, qbuf, local_sem.at[0]),
        pltpu.make_async_copy(k_ref.at[:, pl.ds(own_cols, HCOLS)], kbuf.at[own], kv_recv.at[0]),
        pltpu.make_async_copy(v_ref.at[:, pl.ds(own_cols, HCOLS)], vbuf.at[own], kv_recv.at[1]),
        pltpu.make_async_copy(w_ref, wbuf.at[row], local_sem.at[3]),
        pltpu.make_async_copy(res_ref, rbuf, local_sem.at[4]),
    ]
    for copy in locals_:
        copy.start()
    pl.semaphore_wait(barrier, len(partners) + len(around))

    def owner(dx, dy):
        return ((x + dx) % NX) * NY + (y + dy) % NY

    def w_copy(i, arrived):
        axis, sign, dx, dy, lo, hi = MESSAGES[i]
        if arrived:
            dx, dy = (dx - sign, dy) if axis == 0 else (dx, dy - sign)
        slot = wbuf.at[owner(dx, dy), pl.ds(lo, hi - lo), :]
        mine = not arrived and dx == 0 and dy == 0
        return pltpu.make_async_remote_copy(
            src_ref=w_ref.at[pl.ds(lo, hi - lo), :] if mine else slot,
            dst_ref=slot,
            send_sem=w_send,
            recv_sem=w_recv.at[i],
            device_id=(at_xy(axis, sign), tp),
            device_id_type=MESH,
        )

    def send_kv(which):
        src, dst = ((k_ref, kbuf), (v_ref, vbuf))[which]
        for _, to in partners[1:] + partners[:1]:
            pltpu.make_async_remote_copy(
                src_ref=src.at[:, pl.ds(pl.multiple_of(to * HCOLS, HCOLS), HCOLS)],
                dst_ref=dst.at[own],
                send_sem=kv_send.at[which],
                recv_sem=kv_recv.at[which],
                device_id=(row, to),
                device_id_type=MESH,
            ).start()

    for i in FIRST:
        w_copy(i, False).start()
    send_kv(0)
    send_kv(1)
    def kv_wait(which):
        buf = (kbuf, vbuf)[which]
        pltpu.make_async_copy(buf, buf, kv_recv.at[which]).wait()
    def score(span):
        rows = pl.ds(span * CH, CH)
        keys = [kbuf[idx_ref[k, span]] for k in range(2)]
        for h in range(HEADS):
            query = qbuf[rows, h * HD:(h + 1) * HD]
            raw = jnp.concatenate(
                [
                    lax.dot_general(
                        query, block[:, h * HD:(h + 1) * HD], (((1,), (1,)), ((), ())),
                        preferred_element_type=F32,
                    )
                    for block in keys
                ],
                axis=1,
            ) * (1.0 / math.sqrt(HD))
            weights = jnp.exp(raw - jnp.max(raw, axis=1, keepdims=True))
            total = jnp.sum(weights, axis=1, keepdims=True)
            probs[rows, h * 2 * R:(h + 1) * 2 * R] = (weights / total).astype(BF16)

    def attend(span):
        rows = pl.ds(span * CH, CH)
        values = [vbuf[idx_ref[k, span]] for k in range(2)]
        for h in range(HEADS):
            value = jnp.concatenate([block[:, h * HD:(h + 1) * HD] for block in values], axis=0)
            out = jnp.dot(probs[rows, h * 2 * R:(h + 1) * 2 * R], value, preferred_element_type=F32)
            attn[rows, h * HD:(h + 1) * HD] = out.astype(BF16)

    locals_[0].wait()
    fetch.wait()
    scored = False
    late = []
    for now, i, sends, last in STEPS:
        if now > SCORE_AT and not scored:
            scored = True
            kv_wait(0)
            for span in range(SPANS):
                score(span)
        if last:
            late.append(i)
            continue
        w_copy(i, True).wait_recv()
        for j in sends:
            w_copy(j, False).start()
    if not scored:
        kv_wait(0)
        for span in range(SPANS):
            score(span)
    kv_wait(1)
    for span in range(SPANS):
        attend(span)
    for copy in locals_[3:]:
        copy.wait()

    def block_of(side, g, j):
        (ax, ay), (bx, by) = (ORDER[(g * 2 + s) * GB + j] for s in range(2))
        return owner(ax + side * (bx - ax), ay + side * (by - ay))

    def arrived(g):
        for i in late:
            if place(i) // (2 * GB) == g:
                w_copy(i, True).wait_recv()

    def tokens_of(dz, rows=TOKZ, base=0):
        return pl.ds(pl.multiple_of(((z + dz) % NZ) * TOKZ + base, rows), rows)

    def remote(src, dst, send, recv, to):
        return pltpu.make_async_remote_copy(
            src_ref=src, dst_ref=dst, send_sem=send, recv_sem=recv, device_id=(row, to), device_id_type=MESH
        )

    def chain(g, step, way):
        buf = chains.at[way, g]
        if step == 0:
            cols = pl.ds(way * (GC // 2), GC // 2)
            src, dst = sbuf.at[g, tokens_of(4), cols], buf.at[0, :, cols]
        else:
            src, dst = buf.at[step - 1], buf.at[step]
        return remote(src, dst, c_send.at[way, g, step], c_recv.at[way, g, step], at_z(1 - 2 * way))

    def last_hop(g, way, dc):
        rows = pl.ds(pl.multiple_of(((core + dc) % 2) * TOKD, TOKD), TOKD)
        return remote(
            chains.at[way, g, 2, rows], ends.at[way, dc, g],
            e_send.at[way, dc, g], e_recv.at[way, dc, g], at_z(1 - 2 * way, dc),
        )

    def exchange(g):
        return remote(xsend.at[g], xrecv.at[g], x_send.at[g], x_recv.at[g], sibling)

    def share(g):
        src = sbuf.at[g, tokens_of(0, TOKD, (1 - core) * TOKD)]
        return remote(src, shared.at[g], s_send.at[g], s_recv.at[g], sibling)

    def project(g):
        arrived(g)
        for other in (True, False):
            side = 1 - core if other else core
            for j in range(GB):
                part = jnp.dot(attn[...], wbuf[block_of(side, g, j)], preferred_element_type=F32)
                cols = slice(j * WCOLS, (j + 1) * WCOLS)
                if other:
                    xsend[g, :, cols] = part.astype(BF16)
                else:
                    pown[g, :, cols] = part
            if other:
                exchange(g).start()

    def combine(g):
        exchange(g).wait_recv()
        sbuf[g] = (pown[g] + xrecv[g].astype(F32)).astype(BF16)
        for way in range(2):
            chain(g, 0, way).start()
        share(g).start()

    def relay(g, step):
        for way in range(2):
            chain(g, step - 1, way).wait_recv()
            buf = chains.at[way, g, step - 1]
            tokens = tokens_of((1 - 2 * way) * (4 - step))
            if step == 1:
                cut = GC // 2
                got, rest = slice(way * cut, (way + 1) * cut), slice((1 - way) * cut, (2 - way) * cut)
                buf[:, got] = (buf[:, got].astype(F32) + sbuf[g, tokens, got].astype(F32)).astype(BF16)
                buf[:, rest] = sbuf[g, tokens, rest]
            else:
                buf[...] = (buf[...].astype(F32) + sbuf[g, tokens, :].astype(F32)).astype(BF16)
            if step < 3:
                chain(g, step, way).start()
            else:
                for dc in (1, 0):
                    last_hop(g, way, dc).start()

    def finish(g):
        share(g).wait_recv()
        for way in range(2):
            for dc in range(2):
                last_hop(g, way, dc).wait_recv()
        mine = tokens_of(0, TOKD, core * TOKD)
        for dc in range(2):
            side = core if dc == 0 else 1 - core
            for j in range(GB):
                at = pl.ds(pl.multiple_of(block_of(side, g, j) * WCOLS, WCOLS), WCOLS)
                cols = slice(j * WCOLS, (j + 1) * WCOLS)
                here = sbuf[g, mine, cols] if dc == 0 else shared[g, :, cols]
                out_ref[:, at] = (
                    rbuf[:, at].astype(F32)
                    + here.astype(F32)
                    + ends[0, dc, g, :, cols].astype(F32)
                    + ends[1, dc, g, :, cols].astype(F32)
                ).astype(BF16)

    for what, g, step in SUMS:
        if what == 0:
            project(g)
        elif what == 1:
            combine(g)
        elif what == 2:
            relay(g, step)
        else:
            finish(g)
    for g in range(G):
        exchange(g).wait_send()
        share(g).wait_send()
        for way in range(2):
            for step in range(3):
                chain(g, step, way).wait_send()
            for dc in range(2):
                last_hop(g, way, dc).wait_send()
    waitbuf = wbuf.at[pl.ds(0, TP - 1), pl.ds(0, KROWS * HCOLS // WCOLS), :]
    for which in range(2):
        pltpu.make_async_copy(waitbuf, waitbuf, kv_send.at[which]).wait()
    rest = wbuf.at[pl.ds(0, ROWS - 1)]
    pltpu.make_async_copy(rest, rest, w_send).wait()


def solution(mesh):
    def shards(queries, nbr_keys, nbr_values, nbr_index, residual, out_weight):
        hbm = pl.BlockSpec(memory_space=pl.ANY)
        dma = pltpu.SemaphoreType.DMA
        return pl.pallas_call(
            kernel,
            out_shape=jax.ShapeDtypeStruct((TOKD, D), BF16),
            in_specs=[hbm] * 6,
            out_specs=pl.BlockSpec(memory_space=pltpu.VMEM),
            scratch_shapes=[
                pltpu.SMEM((2, SPANS), jnp.int32),
                pltpu.VMEM((NZ, R, HCOLS), BF16),
                pltpu.VMEM((NZ, R, HCOLS), BF16),
                pltpu.VMEM((TOK, HCOLS), BF16),
                pltpu.VMEM((TOKD, D), BF16),
                pltpu.VMEM((ROWS, HCOLS, WCOLS), BF16),
                pltpu.VMEM((TOK, HCOLS), BF16),
                pltpu.VMEM((TOK, HEADS * 2 * R), BF16),
                pltpu.VMEM((G, TOK, GC), BF16),
                pltpu.VMEM((G, TOK, GC), BF16),
                pltpu.VMEM((G, TOK, GC), F32),
                pltpu.VMEM((G, TOK, GC), BF16),
                pltpu.VMEM((G, TOKD, GC), BF16),
                pltpu.VMEM((2, G, 3, TOKZ, GC), BF16),
                pltpu.VMEM((2, 2, G, TOKD, GC), BF16),
                dma, dma((5,)), dma((2,)), dma((2,)), dma, dma((len(MESSAGES),)),
                dma((G,)), dma((G,)), dma((G,)), dma((G,)),
                dma((2, G, 3)), dma((2, G, 3)), dma((2, 2, G)), dma((2, 2, G)),
            ],
            compiler_params=pltpu.CompilerParams(
                collective_id=0, has_side_effects=True, vmem_limit_bytes=56 * 1024 * 1024
            ),
            cost_estimate=pl.CostEstimate(flops=2_400_000_000, bytes_accessed=12_000_000, transcendentals=262144),
        )(nbr_index.T, queries, nbr_keys, nbr_values, residual, out_weight)

    placed = (
        P("rows", "tp"),
        P(("rows", "tp"), None),
        P(("rows", "tp"), None),
        P("rows", None),
        P(("rows", "tp"), None),
        P("tp", "rows"),
    )
    return jax.shard_map(
        shards, mesh=mesh, in_specs=placed, out_specs=P(("rows", "tp"), None), check_vma=False
    )
```

```python
import heapq
import math

import jax
import jax.numpy as jnp
from jax import lax
from jax.experimental import pallas as pl
from jax.experimental.pallas import tpu as pltpu
from jax.sharding import PartitionSpec as P

MESH = pl.DeviceIdType.MESH
F32, BF16 = jnp.float32, jnp.bfloat16

HD, CH, R = 128, 64, 128
NX, NY, NZ = 4, 8, 8
TP, ROWS = 16, 32
TOK, HCOLS, WCOLS, KROWS = 256, 512, 256, 64
D = 8192
SPANS, HEADS = TOK // CH, HCOLS // HD
TOKZ, TOKD = TOK // NZ, TOK // TP
HALF = D // 2
G = 4
GC = HALF // G
GB = GC // WCOLS

PIECES = ((4,), (3, -3, 2, -2), (1, -1, 0))

PARTS = ((0, 208, 112), (208, 512, 352))

SCORE_AT = 30.0


def gather_plan():
    messages, needs = [], []

    def add(part, axis, sign, dx, dy, piece, need):
        lo, hi, mid = PARTS[part]
        lo, hi = ((lo, hi), (lo, mid), (mid, hi))[piece]
        messages.append((axis, sign, dx, dy, lo, hi))
        needs.append(need)
        return len(messages) - 1

    def ring(part, axis, size, other, need):
        got = {0: need}
        for sign in (1, -1):
            for step in range(size // 2):
                at = -sign * step
                last = step == size // 2 - 1
                piece = 0 if not last else (1 if sign == 1 else 2)
                dx, dy = (at, other) if axis == 0 else (other, at)
                bring = add(part, axis, sign, dx, dy, piece, got[at])
                key = size // 2 if last else at - sign
                got[key] = got.get(key, ()) + (bring,) if last else (bring,)
        return got

    for bx, need in ring(0, 0, NX, 0, ()).items():
        ring(0, 1, NY, bx, need)
    for by, need in ring(1, 1, NY, 0, ()).items():
        ring(1, 0, NX, by, need)

    count = len(messages)
    feeds = [[j for j in range(count) if i in needs[j]] for i in range(count)]
    depth = [0] * count
    for i in reversed(range(count)):
        depth[i] = max([1 + depth[j] for j in feeds[i]], default=0)
    rate, delay = 2 * WCOLS * 2 / 90e3, 1.5
    free = {}
    queue = []
    left = [len(n) for n in needs]

    def launch(i, now):
        axis, sign, _, _, lo, hi = messages[i]
        begin = max(now, free.get((axis, sign), 0.0))
        free[axis, sign] = begin + (hi - lo) * rate
        heapq.heappush(queue, (free[axis, sign] + delay, i))

    first = sorted((i for i in range(count) if not needs[i]), key=lambda i: (-depth[i], i))
    for i in first:
        launch(i, 0.0)
    steps = []
    while queue:
        now, i = heapq.heappop(queue)
        ready = []
        for j in feeds[i]:
            left[j] -= 1
            if left[j] == 0:
                ready.append(j)
        ready.sort(key=lambda j: (-depth[j], j))
        for j in ready:
            launch(j, now)
        steps.append((now, i, ready, not feeds[i]))
    return messages, first, steps


MESSAGES, FIRST, STEPS = gather_plan()


def wrap(axis, d):
    size = (NX, NY)[axis]
    return (d + size // 2 - 1) % size - (size // 2 - 1)


def came(i):
    axis, sign, dx, dy, _, _ = MESSAGES[i]
    return (wrap(0, dx - sign), wrap(1, dy)) if axis == 0 else (wrap(0, dx), wrap(1, dy - sign))


def arrival_order():
    when = {(0, 0): 0.0}
    for now, i, _, _ in STEPS:
        when[came(i)] = now
    return sorted(when, key=lambda at: (when[at], at))


ORDER = arrival_order()


def turns():
    passed = [(now, i, sends) for now, i, sends, last in STEPS if not last]
    chunk = {i: ORDER.index(came(i)) // (2 * GB) for _, i, _, _ in STEPS}
    signal = {i: n for n, (_, i, _) in enumerate(passed)}
    sizes, own = [], len(passed) + G
    for g in range(G):
        rest, alone, fits = [i for _, i, _, last in STEPS if last and chunk[i] == g], [], []
        while rest and not fits:
            total = sum(MESSAGES[i][5] - MESSAGES[i][4] for i in rest)
            fits = [k for k in range(1, ROWS) if total % (16 * k) == 0 and total // k <= HCOLS]
            if not fits:
                alone.append(rest.pop())
        signal.update({i: len(passed) + g for i in rest})
        signal.update({i: own + n for n, i in enumerate(alone)})
        own += len(alone)
        sizes.append(((fits[0], total // fits[0]) if rest else None, alone))
    return passed, signal, sizes, own


TURNS, SIGNAL, LATE, W_SEMS = turns()


def sum_plan():
    project_us, meet_us, small_us, link_us, delay_us = 2.4 / G, 1.3, 0.25, 5.8 / G, 1.6
    now, free = 0.0, 0.0
    ready = []
    order, left = [], list(range(G))
    while left or ready:
        able = sorted((-stage, g) for t, stage, g in ready if t <= now)
        if able:
            stage, g = -able[0][0], able[0][1]
            ready = [r for r in ready if r[1:] != (stage, g)]
            now += small_us
            order.append((1, g, 0) if stage == 0 else (2, g, stage) if stage < 4 else (3, g, 0))
            if stage < 4:
                free = max(now, free) + link_us * (0.5 if stage == 0 else 1.0)
                ready.append((free + delay_us, stage + 1, g))
        elif left:
            g = left.pop(0)
            order.append((0, g, 0))
            ready.append((now + project_us / 2 + meet_us, 0, g))
            now += project_us
        else:
            now = min(t for t, _, _ in ready)
    return order, now


SUMS, SUMS_US = sum_plan()


def kernel(
    idx_hbm, q_ref, k_ref, v_ref, res_ref, w_ref, out_ref,
    idx_ref, kbuf, vbuf, qbuf, rbuf, wbuf, attn, probs, xsend, xrecv, pown, first, last, shared, chains, ends,
    idx_sem, local_sem, kv_send, kv_recv, w_send, w_recv,
    x_send, x_recv, s_send, s_recv, c_send, c_recv, e_send, e_recv,
):
    row, tp = lax.axis_index("rows"), lax.axis_index("tp")
    x, y = row // NY, row % NY
    z, core = tp // 2, tp % 2
    sibling = z * 2 + (1 - core)

    def at_z(dz, dc=0):
        return ((z + dz) % NZ) * 2 + (core + dc) % 2

    def at_xy(axis, sign):
        if axis == 0:
            return ((x + sign) % NX) * NY + y
        return x * NY + (y + sign) % NY

    partners = [(row, sibling)]
    partners += [(row, at_z(dz, dc)) for dz in (4, 3, -3, 2, -2, 1, -1) for dc in (0, 1)]
    around = [(at_xy(axis, sign), tp) for axis in (0, 1) for sign in (1, -1)]

    barrier = pltpu.get_barrier_semaphore()
    for who in partners + around:
        pl.semaphore_signal(barrier, inc=1, device_id=who, device_id_type=MESH)

    own = (z, pl.ds(pl.multiple_of(core * KROWS, KROWS), KROWS))
    own_cols = pl.multiple_of(tp * HCOLS, HCOLS)

    fetch = pltpu.make_async_copy(idx_hbm, idx_ref, idx_sem)
    fetch.start()
    locals_ = [
        pltpu.make_async_copy(q_ref, qbuf, local_sem.at[0]),
        pltpu.make_async_copy(k_ref.at[:, pl.ds(own_cols, HCOLS)], kbuf.at[own], kv_recv.at[0]),
        pltpu.make_async_copy(v_ref.at[:, pl.ds(own_cols, HCOLS)], vbuf.at[own], kv_recv.at[1]),
        pltpu.make_async_copy(w_ref, wbuf.at[row], local_sem.at[3]),
        pltpu.make_async_copy(res_ref, rbuf, local_sem.at[4]),
    ]
    for copy in locals_:
        copy.start()
    pl.semaphore_wait(barrier, len(partners) + len(around))

    def owner(dx, dy):
        return ((x + dx) % NX) * NY + (y + dy) % NY

    def w_copy(i, arrived):
        axis, sign, dx, dy, lo, hi = MESSAGES[i]
        if arrived:
            dx, dy = (dx - sign, dy) if axis == 0 else (dx, dy - sign)
        slot = wbuf.at[owner(dx, dy), pl.ds(lo, hi - lo), :]
        mine = not arrived and dx == 0 and dy == 0
        return pltpu.make_async_remote_copy(
            src_ref=w_ref.at[pl.ds(lo, hi - lo), :] if mine else slot,
            dst_ref=slot,
            send_sem=w_send,
            recv_sem=w_recv.at[SIGNAL[i]],
            device_id=(at_xy(axis, sign), tp),
            device_id_type=MESH,
        )

    def send_kv(which):
        src, dst = ((k_ref, kbuf), (v_ref, vbuf))[which]
        for _, to in partners[1:] + partners[:1]:
            pltpu.make_async_remote_copy(
                src_ref=src.at[:, pl.ds(pl.multiple_of(to * HCOLS, HCOLS), HCOLS)],
                dst_ref=dst.at[own],
                send_sem=kv_send.at[which],
                recv_sem=kv_recv.at[which],
                device_id=(row, to),
                device_id_type=MESH,
            ).start()

    for i in FIRST:
        w_copy(i, False).start()
    send_kv(0)
    send_kv(1)
    def kv_wait(which):
        buf = (kbuf, vbuf)[which]
        pltpu.make_async_copy(buf, buf, kv_recv.at[which]).wait()
    def score(span):
        rows = pl.ds(span * CH, CH)
        keys = [kbuf[idx_ref[k, span]] for k in range(2)]
        for h in range(HEADS):
            query = qbuf[rows, h * HD:(h + 1) * HD]
            raw = jnp.concatenate(
                [
                    lax.dot_general(
                        query, block[:, h * HD:(h + 1) * HD], (((1,), (1,)), ((), ())),
                        preferred_element_type=F32,
                    )
                    for block in keys
                ],
                axis=1,
            ) * (1.0 / math.sqrt(HD))
            weights = jnp.exp(raw - jnp.max(raw, axis=1, keepdims=True))
            total = jnp.sum(weights, axis=1, keepdims=True)
            probs[rows, h * 2 * R:(h + 1) * 2 * R] = (weights / total).astype(BF16)

    def attend(span):
        rows = pl.ds(span * CH, CH)
        values = [vbuf[idx_ref[k, span]] for k in range(2)]
        for h in range(HEADS):
            value = jnp.concatenate([block[:, h * HD:(h + 1) * HD] for block in values], axis=0)
            out = jnp.dot(probs[rows, h * 2 * R:(h + 1) * 2 * R], value, preferred_element_type=F32)
            attn[rows, h * HD:(h + 1) * HD] = out.astype(BF16)

    locals_[0].wait()
    fetch.wait()
    turn = 0

    def pump(until):
        nonlocal turn
        while turn < len(TURNS) and TURNS[turn][0] < until:
            _, i, sends = TURNS[turn]
            w_copy(i, True).wait_recv()
            for j in sends:
                w_copy(j, False).start()
            turn += 1

    pump(SCORE_AT)
    kv_wait(0)
    for span in range(SPANS):
        score(span)
    pump(math.inf)
    kv_wait(1)
    for span in range(SPANS):
        attend(span)
    for copy in locals_[3:]:
        copy.wait()

    def block_of(side, g, j):
        (ax, ay), (bx, by) = (ORDER[(g * 2 + s) * GB + j] for s in range(2))
        return owner(ax + side * (bx - ax), ay + side * (by - ay))

    def arrived(g):
        shared_size, alone = LATE[g]
        for i in alone:
            w_copy(i, True).wait_recv()
        if shared_size:
            count, rows = shared_size
            part = wbuf.at[pl.ds(0, count), pl.ds(0, rows), :]
            pltpu.make_async_copy(part, part, w_recv.at[len(TURNS) + g]).wait()

    def tokens_of(dz, rows=TOKZ, base=0):
        return pl.ds(pl.multiple_of(((z + dz) % NZ) * TOKZ + base, rows), rows)

    def remote(src, dst, send, recv, to):
        return pltpu.make_async_remote_copy(
            src_ref=src, dst_ref=dst, send_sem=send, recv_sem=recv, device_id=(row, to), device_id_type=MESH
        )

    def chain(g, step, way):
        buf = chains.at[way, g]
        if step == 0:
            cols = pl.ds(way * (GC // 2), GC // 2)
            src, dst = first.at[g, :, cols], buf.at[0, :, cols]
        else:
            src, dst = buf.at[step - 1], buf.at[step]
        return remote(src, dst, c_send, c_recv.at[way, g, step], at_z(1 - 2 * way))

    def last_hop(g, way, dc):
        rows = pl.ds(pl.multiple_of(((core + dc) % 2) * TOKD, TOKD), TOKD)
        return remote(
            chains.at[way, g, 2, rows], ends.at[g, way, dc],
            e_send, e_recv.at[g], at_z(1 - 2 * way, dc),
        )

    def exchange(g, piece):
        for dz in PIECES[piece]:
            rows = tokens_of(dz)
            remote(xsend.at[g, rows], xrecv.at[g, rows], x_send, x_recv.at[g, piece], sibling).start()

    def met(g, piece):
        part = xrecv.at[g, pl.ds(0, len(PIECES[piece]) * TOKZ)]
        pltpu.make_async_copy(part, part, x_recv.at[g, piece]).wait()

    def both(g, rows, cols=slice(None)):
        return pown[g, rows, cols] + xrecv[g, rows, cols].astype(F32)

    def share(g):
        return remote(last.at[g], shared.at[g], s_send, s_recv.at[g], sibling)

    def project(g):
        arrived(g)
        for other in (True, False):
            side = 1 - core if other else core
            for j in range(GB):
                part = jnp.dot(attn[...], wbuf[block_of(side, g, j)], preferred_element_type=F32)
                cols = slice(j * WCOLS, (j + 1) * WCOLS)
                if other:
                    xsend[g, :, cols] = part.astype(BF16)
                else:
                    pown[g, :, cols] = part
            if other:
                exchange(g, 0)

    def start(g):
        met(g, 0)
        first[g] = both(g, tokens_of(4)).astype(BF16)
        for way in range(2):
            chain(g, 0, way).start()
        exchange(g, 1)
        exchange(g, 2)

    def relay(g, step):
        if step != 2:
            met(g, 1 if step == 1 else 2)
        for way in range(2):
            chain(g, step - 1, way).wait_recv()
            buf = chains.at[way, g, step - 1]
            tokens = tokens_of((1 - 2 * way) * (4 - step))
            if step == 1:
                cut = GC // 2
                got, rest = slice(way * cut, (way + 1) * cut), slice((1 - way) * cut, (2 - way) * cut)
                buf[:, got] = (buf[:, got].astype(F32) + both(g, tokens, got)).astype(BF16)
                buf[:, rest] = both(g, tokens, rest).astype(BF16)
            else:
                buf[...] = (buf[...].astype(F32) + both(g, tokens)).astype(BF16)
            if step < 3:
                chain(g, step, way).start()
            else:
                for dc in (1, 0):
                    last_hop(g, way, dc).start()
        if step == 3:
            last[g] = both(g, tokens_of(0, TOKD, (1 - core) * TOKD)).astype(BF16)
            share(g).start()

    def finish(g):
        share(g).wait_recv()
        pltpu.make_async_copy(ends.at[g], ends.at[g], e_recv.at[g]).wait()
        mine = tokens_of(0, TOKD, core * TOKD)
        for dc in range(2):
            side = core if dc == 0 else 1 - core
            for j in range(GB):
                at = pl.ds(pl.multiple_of(block_of(side, g, j) * WCOLS, WCOLS), WCOLS)
                cols = slice(j * WCOLS, (j + 1) * WCOLS)
                here = both(g, mine, cols) if dc == 0 else shared[g, :, cols].astype(F32)
                out_ref[:, at] = (
                    rbuf[:, at].astype(F32)
                    + here
                    + ends[g, 0, dc, :, cols].astype(F32)
                    + ends[g, 1, dc, :, cols].astype(F32)
                ).astype(BF16)

    for what, g, step in SUMS:
        if what == 0:
            project(g)
        elif what == 1:
            start(g)
        elif what == 2:
            relay(g, step)
        else:
            finish(g)
    sent = wbuf.at[pl.ds(0, 2 * G * 5 * GB * TOKZ // 2 // HCOLS)]
    for part, sem in ((xsend, x_send), (shared, s_send), (ends, e_send), (sent, c_send)):
        pltpu.make_async_copy(part, part, sem).wait()
    waitbuf = wbuf.at[pl.ds(0, TP - 1), pl.ds(0, KROWS * HCOLS // WCOLS), :]
    for which in range(2):
        pltpu.make_async_copy(waitbuf, waitbuf, kv_send.at[which]).wait()
    rest = wbuf.at[pl.ds(0, ROWS - 1)]
    pltpu.make_async_copy(rest, rest, w_send).wait()


def solution(mesh):
    def shards(queries, nbr_keys, nbr_values, nbr_index, residual, out_weight):
        hbm = pl.BlockSpec(memory_space=pl.ANY)
        dma = pltpu.SemaphoreType.DMA
        return pl.pallas_call(
            kernel,
            out_shape=jax.ShapeDtypeStruct((TOKD, D), BF16),
            in_specs=[hbm] * 6,
            out_specs=pl.BlockSpec(memory_space=pltpu.VMEM),
            scratch_shapes=[
                pltpu.SMEM((2, SPANS), jnp.int32),
                pltpu.VMEM((NZ, R, HCOLS), BF16),
                pltpu.VMEM((NZ, R, HCOLS), BF16),
                pltpu.VMEM((TOK, HCOLS), BF16),
                pltpu.VMEM((TOKD, D), BF16),
                pltpu.VMEM((ROWS, HCOLS, WCOLS), BF16),
                pltpu.VMEM((TOK, HCOLS), BF16),
                pltpu.VMEM((TOK, HEADS * 2 * R), BF16),
                pltpu.VMEM((G, TOK, GC), BF16),
                pltpu.VMEM((G, TOK, GC), BF16),
                pltpu.VMEM((G, TOK, GC), F32),
                pltpu.VMEM((G, TOKZ, GC), BF16),
                pltpu.VMEM((G, TOKD, GC), BF16),
                pltpu.VMEM((G, TOKD, GC), BF16),
                pltpu.VMEM((2, G, 3, TOKZ, GC), BF16),
                pltpu.VMEM((G, 2, 2, TOKD, GC), BF16),
                dma, dma((5,)), dma((2,)), dma((2,)), dma, dma((W_SEMS,)),
                dma, dma((G, len(PIECES))), dma, dma((G,)), dma, dma((2, G, 3)), dma, dma((G,)),
            ],
            compiler_params=pltpu.CompilerParams(
                collective_id=0, has_side_effects=True, vmem_limit_bytes=56 * 1024 * 1024
            ),
            cost_estimate=pl.CostEstimate(flops=2_400_000_000, bytes_accessed=12_000_000, transcendentals=262144),
        )(nbr_index.T, queries, nbr_keys, nbr_values, residual, out_weight)

    placed = (
        P("rows", "tp"),
        P(("rows", "tp"), None),
        P(("rows", "tp"), None),
        P("rows", None),
        P(("rows", "tp"), None),
        P("tp", "rows"),
    )
    return jax.shard_map(
        shards, mesh=mesh, in_specs=placed, out_specs=P(("rows", "tp"), None), check_vma=False
    )
```

```python
import heapq
import math

import jax
import jax.numpy as jnp
from jax import lax
from jax.experimental import pallas as pl
from jax.experimental.pallas import tpu as pltpu
from jax.sharding import PartitionSpec as P

MESH = pl.DeviceIdType.MESH
F32, BF16 = jnp.float32, jnp.bfloat16

HD, CH, R = 128, 64, 128
NX, NY, NZ = 4, 8, 8
TP, ROWS = 16, 32
TOK, HCOLS, WCOLS, KROWS = 256, 512, 256, 64
D = 8192
SPANS, HEADS = TOK // CH, HCOLS // HD
TOKZ, TOKD = TOK // NZ, TOK // TP
HALF = D // 2
G = 4
GC = HALF // G
GB = GC // WCOLS

SCORE_STEP = 1.5

PIECES = ((4,), (3, -3, 2, -2), (1, -1, 0))

PARTS = ((0, 208, 112), (208, 512, 352))

SCORE_AT = 36.0


def gather_plan():
    messages, needs = [], []

    def add(part, axis, sign, dx, dy, piece, need):
        lo, hi, mid = PARTS[part]
        lo, hi = ((lo, hi), (lo, mid), (mid, hi))[piece]
        messages.append((axis, sign, dx, dy, lo, hi))
        needs.append(need)
        return len(messages) - 1

    def ring(part, axis, size, other, need):
        got = {0: need}
        for sign in (1, -1):
            for step in range(size // 2):
                at = -sign * step
                last = step == size // 2 - 1
                piece = 0 if not last else (1 if sign == 1 else 2)
                dx, dy = (at, other) if axis == 0 else (other, at)
                bring = add(part, axis, sign, dx, dy, piece, got[at])
                key = size // 2 if last else at - sign
                got[key] = got.get(key, ()) + (bring,) if last else (bring,)
        return got

    for bx, need in ring(0, 0, NX, 0, ()).items():
        ring(0, 1, NY, bx, need)
    for by, need in ring(1, 1, NY, 0, ()).items():
        ring(1, 0, NX, by, need)

    count = len(messages)
    feeds = [[j for j in range(count) if i in needs[j]] for i in range(count)]
    depth = [0] * count
    for i in reversed(range(count)):
        depth[i] = max([1 + depth[j] for j in feeds[i]], default=0)
    rate, delay = 2 * WCOLS * 2 / 90e3, 1.5
    free = {}
    queue = []
    left = [len(n) for n in needs]

    def launch(i, now):
        axis, sign, _, _, lo, hi = messages[i]
        begin = max(now, free.get((axis, sign), 0.0))
        free[axis, sign] = begin + (hi - lo) * rate
        heapq.heappush(queue, (free[axis, sign] + delay, i))

    first = sorted((i for i in range(count) if not needs[i]), key=lambda i: (-depth[i], i))
    for i in first:
        launch(i, 0.0)
    steps = []
    while queue:
        now, i = heapq.heappop(queue)
        ready = []
        for j in feeds[i]:
            left[j] -= 1
            if left[j] == 0:
                ready.append(j)
        ready.sort(key=lambda j: (-depth[j], j))
        for j in ready:
            launch(j, now)
        steps.append((now, i, ready, not feeds[i]))
    return messages, first, steps


MESSAGES, FIRST, STEPS = gather_plan()


def wrap(axis, d):
    size = (NX, NY)[axis]
    return (d + size // 2 - 1) % size - (size // 2 - 1)


def came(i):
    axis, sign, dx, dy, _, _ = MESSAGES[i]
    return (wrap(0, dx - sign), wrap(1, dy)) if axis == 0 else (wrap(0, dx), wrap(1, dy - sign))


def arrival_order():
    when = {(0, 0): 0.0}
    for now, i, _, _ in STEPS:
        when[came(i)] = now
    return sorted(when, key=lambda at: (when[at], at))


ORDER = arrival_order()


def turns():
    passed = [(now, i, sends) for now, i, sends, last in STEPS if not last]
    chunk = {i: ORDER.index(came(i)) // (2 * GB) for _, i, _, _ in STEPS}
    signal = {i: n for n, (_, i, _) in enumerate(passed)}
    sizes, own = [], len(passed) + G
    for g in range(G):
        rest, alone, fits = [i for _, i, _, last in STEPS if last and chunk[i] == g], [], []
        while rest and not fits:
            total = sum(MESSAGES[i][5] - MESSAGES[i][4] for i in rest)
            fits = [k for k in range(1, ROWS) if total % (16 * k) == 0 and total // k <= HCOLS]
            if not fits:
                alone.append(rest.pop())
        signal.update({i: len(passed) + g for i in rest})
        signal.update({i: own + n for n, i in enumerate(alone)})
        own += len(alone)
        sizes.append(((fits[0], total // fits[0]) if rest else None, alone))
    return passed, signal, sizes, own


TURNS, SIGNAL, LATE, W_SEMS = turns()


def sum_plan():
    project_us, meet_us, small_us, link_us, delay_us = 2.4 / G, 1.3, 0.25, 5.8 / G, 1.6
    now, free = 0.0, 0.0
    ready = []
    order, left = [], list(range(G))
    while left or ready:
        able = sorted((-stage, g) for t, stage, g in ready if t <= now)
        if able:
            stage, g = -able[0][0], able[0][1]
            ready = [r for r in ready if r[1:] != (stage, g)]
            now += small_us
            order.append((1, g, 0) if stage == 0 else (2, g, stage) if stage < 4 else (3, g, 0))
            if stage < 4:
                free = max(now, free) + link_us * (0.5 if stage == 0 else 1.0)
                ready.append((free + delay_us, stage + 1, g))
        elif left:
            g = left.pop(0)
            order.append((0, g, 0))
            ready.append((now + project_us / 2 + meet_us, 0, g))
            now += project_us
        else:
            now = min(t for t, _, _ in ready)
    return order, now


SUMS, SUMS_US = sum_plan()


def kernel(
    idx_hbm, q_ref, k_ref, v_ref, res_ref, w_ref, out_ref,
    idx_ref, kbuf, vbuf, qbuf, rbuf, wbuf, attn, probs, xsend, xrecv, pown, first, last, shared, chains, ends,
    idx_sem, local_sem, kv_send, kv_recv, w_send, w_recv,
    x_send, x_recv, s_send, s_recv, c_send, c_recv, e_send, e_recv,
):
    row, tp = lax.axis_index("rows"), lax.axis_index("tp")
    x, y = row // NY, row % NY
    z, core = tp // 2, tp % 2
    sibling = z * 2 + (1 - core)

    def at_z(dz, dc=0):
        return ((z + dz) % NZ) * 2 + (core + dc) % 2

    def at_xy(axis, sign):
        if axis == 0:
            return ((x + sign) % NX) * NY + y
        return x * NY + (y + sign) % NY

    partners = [(row, sibling)]
    partners += [(row, at_z(dz, dc)) for dz in (4, 3, -3, 2, -2, 1, -1) for dc in (0, 1)]
    around = [(at_xy(axis, sign), tp) for axis in (0, 1) for sign in (1, -1)]

    barrier = pltpu.get_barrier_semaphore()
    for who in partners + around:
        pl.semaphore_signal(barrier, inc=1, device_id=who, device_id_type=MESH)

    own = (z, pl.ds(pl.multiple_of(core * KROWS, KROWS), KROWS))
    own_cols = pl.multiple_of(tp * HCOLS, HCOLS)

    fetch = pltpu.make_async_copy(idx_hbm, idx_ref, idx_sem)
    fetch.start()
    locals_ = [
        pltpu.make_async_copy(q_ref, qbuf, local_sem.at[0]),
        pltpu.make_async_copy(k_ref.at[:, pl.ds(own_cols, HCOLS)], kbuf.at[own], kv_recv.at[0]),
        pltpu.make_async_copy(v_ref.at[:, pl.ds(own_cols, HCOLS)], vbuf.at[own], kv_recv.at[1]),
        pltpu.make_async_copy(w_ref, wbuf.at[row], local_sem.at[3]),
        pltpu.make_async_copy(res_ref, rbuf, local_sem.at[4]),
    ]
    for copy in locals_:
        copy.start()
    pl.semaphore_wait(barrier, len(partners) + len(around))

    def owner(dx, dy):
        return ((x + dx) % NX) * NY + (y + dy) % NY

    def w_copy(i, arrived):
        axis, sign, dx, dy, lo, hi = MESSAGES[i]
        if arrived:
            dx, dy = (dx - sign, dy) if axis == 0 else (dx, dy - sign)
        slot = wbuf.at[owner(dx, dy), pl.ds(lo, hi - lo), :]
        mine = not arrived and dx == 0 and dy == 0
        return pltpu.make_async_remote_copy(
            src_ref=w_ref.at[pl.ds(lo, hi - lo), :] if mine else slot,
            dst_ref=slot,
            send_sem=w_send,
            recv_sem=w_recv.at[SIGNAL[i]],
            device_id=(at_xy(axis, sign), tp),
            device_id_type=MESH,
        )

    def send_kv(which):
        src, dst = ((k_ref, kbuf), (v_ref, vbuf))[which]
        for _, to in partners[1:] + partners[:1]:
            pltpu.make_async_remote_copy(
                src_ref=src.at[:, pl.ds(pl.multiple_of(to * HCOLS, HCOLS), HCOLS)],
                dst_ref=dst.at[own],
                send_sem=kv_send.at[which],
                recv_sem=kv_recv.at[which],
                device_id=(row, to),
                device_id_type=MESH,
            ).start()

    for i in FIRST:
        w_copy(i, False).start()
    send_kv(0)
    send_kv(1)
    def kv_wait(which):
        buf = (kbuf, vbuf)[which]
        pltpu.make_async_copy(buf, buf, kv_recv.at[which]).wait()
    def score(span):
        rows = pl.ds(span * CH, CH)
        keys = [kbuf[idx_ref[k, span]] for k in range(2)]
        for h in range(HEADS):
            query = qbuf[rows, h * HD:(h + 1) * HD]
            raw = jnp.concatenate(
                [
                    lax.dot_general(
                        query, block[:, h * HD:(h + 1) * HD], (((1,), (1,)), ((), ())),
                        preferred_element_type=F32,
                    )
                    for block in keys
                ],
                axis=1,
            ) * (1.0 / math.sqrt(HD))
            weights = jnp.exp(raw - jnp.max(raw, axis=1, keepdims=True))
            total = jnp.sum(weights, axis=1, keepdims=True)
            probs[rows, h * 2 * R:(h + 1) * 2 * R] = (weights / total).astype(BF16)

    def attend(span):
        rows = pl.ds(span * CH, CH)
        values = [vbuf[idx_ref[k, span]] for k in range(2)]
        for h in range(HEADS):
            value = jnp.concatenate([block[:, h * HD:(h + 1) * HD] for block in values], axis=0)
            out = jnp.dot(probs[rows, h * 2 * R:(h + 1) * 2 * R], value, preferred_element_type=F32)
            attn[rows, h * HD:(h + 1) * HD] = out.astype(BF16)

    locals_[0].wait()
    fetch.wait()
    turn = 0

    def pump(until):
        nonlocal turn
        while turn < len(TURNS) and TURNS[turn][0] < until:
            _, i, sends = TURNS[turn]
            w_copy(i, True).wait_recv()
            for j in sends:
                w_copy(j, False).start()
            turn += 1

    pump(SCORE_AT)
    kv_wait(0)
    for span in range(SPANS):
        score(span)
        pump(SCORE_AT + SCORE_STEP * (span + 1))
    pump(math.inf)
    kv_wait(1)
    for span in range(SPANS):
        attend(span)
    for copy in locals_[3:]:
        copy.wait()

    def block_of(side, g, j):
        (ax, ay), (bx, by) = (ORDER[(g * 2 + s) * GB + j] for s in range(2))
        return owner(ax + side * (bx - ax), ay + side * (by - ay))

    def arrived(g):
        shared_size, alone = LATE[g]
        for i in alone:
            w_copy(i, True).wait_recv()
        if shared_size:
            count, rows = shared_size
            part = wbuf.at[pl.ds(0, count), pl.ds(0, rows), :]
            pltpu.make_async_copy(part, part, w_recv.at[len(TURNS) + g]).wait()

    def tokens_of(dz, rows=TOKZ, base=0):
        return pl.ds(pl.multiple_of(((z + dz) % NZ) * TOKZ + base, rows), rows)

    def remote(src, dst, send, recv, to):
        return pltpu.make_async_remote_copy(
            src_ref=src, dst_ref=dst, send_sem=send, recv_sem=recv, device_id=(row, to), device_id_type=MESH
        )

    def chain(g, step, way):
        buf = chains.at[way, g]
        if step == 0:
            cols = pl.ds(way * (GC // 2), GC // 2)
            src, dst = first.at[g, :, cols], buf.at[0, :, cols]
        else:
            src, dst = buf.at[step - 1], buf.at[step]
        return remote(src, dst, c_send, c_recv.at[way, g, step], at_z(1 - 2 * way))

    def last_hop(g, way, dc):
        rows = pl.ds(pl.multiple_of(((core + dc) % 2) * TOKD, TOKD), TOKD)
        return remote(
            chains.at[way, g, 2, rows], ends.at[g, way, dc],
            e_send, e_recv.at[g], at_z(1 - 2 * way, dc),
        )

    def exchange(g, piece):
        for dz in PIECES[piece]:
            rows = tokens_of(dz)
            remote(xsend.at[g, rows], xrecv.at[g, rows], x_send, x_recv.at[g, piece], sibling).start()

    def met(g, piece):
        part = xrecv.at[g, pl.ds(0, len(PIECES[piece]) * TOKZ)]
        pltpu.make_async_copy(part, part, x_recv.at[g, piece]).wait()

    def both(g, rows, cols=slice(None)):
        return pown[g, rows, cols] + xrecv[g, rows, cols].astype(F32)

    def share(g):
        return remote(last.at[g], shared.at[g], s_send, s_recv.at[g], sibling)

    def project(g):
        arrived(g)
        for other in (True, False):
            side = 1 - core if other else core
            for j in range(GB):
                part = jnp.dot(attn[...], wbuf[block_of(side, g, j)], preferred_element_type=F32)
                cols = slice(j * WCOLS, (j + 1) * WCOLS)
                if other:
                    xsend[g, :, cols] = part.astype(BF16)
                else:
                    pown[g, :, cols] = part
            if other:
                exchange(g, 0)

    def start(g):
        met(g, 0)
        first[g] = both(g, tokens_of(4)).astype(BF16)
        for way in range(2):
            chain(g, 0, way).start()
        exchange(g, 1)
        exchange(g, 2)

    def relay(g, step):
        if step != 2:
            met(g, 1 if step == 1 else 2)
        for way in range(2):
            chain(g, step - 1, way).wait_recv()
            buf = chains.at[way, g, step - 1]
            tokens = tokens_of((1 - 2 * way) * (4 - step))
            if step == 1:
                cut = GC // 2
                got, rest = slice(way * cut, (way + 1) * cut), slice((1 - way) * cut, (2 - way) * cut)
                buf[:, got] = (buf[:, got].astype(F32) + both(g, tokens, got)).astype(BF16)
                buf[:, rest] = both(g, tokens, rest).astype(BF16)
            else:
                buf[...] = (buf[...].astype(F32) + both(g, tokens)).astype(BF16)
            if step < 3:
                chain(g, step, way).start()
            else:
                for dc in (1, 0):
                    last_hop(g, way, dc).start()
        if step == 3:
            last[g] = both(g, tokens_of(0, TOKD, (1 - core) * TOKD)).astype(BF16)
            share(g).start()

    def finish(g):
        share(g).wait_recv()
        pltpu.make_async_copy(ends.at[g], ends.at[g], e_recv.at[g]).wait()
        mine = tokens_of(0, TOKD, core * TOKD)
        for dc in range(2):
            side = core if dc == 0 else 1 - core
            for j in range(GB):
                at = pl.ds(pl.multiple_of(block_of(side, g, j) * WCOLS, WCOLS), WCOLS)
                cols = slice(j * WCOLS, (j + 1) * WCOLS)
                here = both(g, mine, cols) if dc == 0 else shared[g, :, cols].astype(F32)
                out_ref[:, at] = (
                    rbuf[:, at].astype(F32)
                    + here
                    + ends[g, 0, dc, :, cols].astype(F32)
                    + ends[g, 1, dc, :, cols].astype(F32)
                ).astype(BF16)

    for what, g, step in SUMS:
        if what == 0:
            project(g)
        elif what == 1:
            start(g)
        elif what == 2:
            relay(g, step)
        else:
            finish(g)
    sent = wbuf.at[pl.ds(0, 2 * G * 5 * GB * TOKZ // 2 // HCOLS)]
    for part, sem in ((xsend, x_send), (shared, s_send), (ends, e_send), (sent, c_send)):
        pltpu.make_async_copy(part, part, sem).wait()
    waitbuf = wbuf.at[pl.ds(0, TP - 1), pl.ds(0, KROWS * HCOLS // WCOLS), :]
    for which in range(2):
        pltpu.make_async_copy(waitbuf, waitbuf, kv_send.at[which]).wait()
    rest = wbuf.at[pl.ds(0, ROWS - 1)]
    pltpu.make_async_copy(rest, rest, w_send).wait()


def solution(mesh):
    def shards(queries, nbr_keys, nbr_values, nbr_index, residual, out_weight):
        hbm = pl.BlockSpec(memory_space=pl.ANY)
        dma = pltpu.SemaphoreType.DMA
        return pl.pallas_call(
            kernel,
            out_shape=jax.ShapeDtypeStruct((TOKD, D), BF16),
            in_specs=[hbm] * 6,
            out_specs=pl.BlockSpec(memory_space=pltpu.VMEM),
            scratch_shapes=[
                pltpu.SMEM((2, SPANS), jnp.int32),
                pltpu.VMEM((NZ, R, HCOLS), BF16),
                pltpu.VMEM((NZ, R, HCOLS), BF16),
                pltpu.VMEM((TOK, HCOLS), BF16),
                pltpu.VMEM((TOKD, D), BF16),
                pltpu.VMEM((ROWS, HCOLS, WCOLS), BF16),
                pltpu.VMEM((TOK, HCOLS), BF16),
                pltpu.VMEM((TOK, HEADS * 2 * R), BF16),
                pltpu.VMEM((G, TOK, GC), BF16),
                pltpu.VMEM((G, TOK, GC), BF16),
                pltpu.VMEM((G, TOK, GC), F32),
                pltpu.VMEM((G, TOKZ, GC), BF16),
                pltpu.VMEM((G, TOKD, GC), BF16),
                pltpu.VMEM((G, TOKD, GC), BF16),
                pltpu.VMEM((2, G, 3, TOKZ, GC), BF16),
                pltpu.VMEM((G, 2, 2, TOKD, GC), BF16),
                dma, dma((5,)), dma((2,)), dma((2,)), dma, dma((W_SEMS,)),
                dma, dma((G, len(PIECES))), dma, dma((G,)), dma, dma((2, G, 3)), dma, dma((G,)),
            ],
            compiler_params=pltpu.CompilerParams(
                collective_id=0, has_side_effects=True, vmem_limit_bytes=56 * 1024 * 1024
            ),
            cost_estimate=pl.CostEstimate(flops=2_400_000_000, bytes_accessed=12_000_000, transcendentals=262144),
        )(nbr_index.T, queries, nbr_keys, nbr_values, residual, out_weight)

    placed = (
        P("rows", "tp"),
        P(("rows", "tp"), None),
        P(("rows", "tp"), None),
        P("rows", None),
        P(("rows", "tp"), None),
        P("tp", "rows"),
    )
    return jax.shard_map(
        shards, mesh=mesh, in_specs=placed, out_specs=P(("rows", "tp"), None), check_vma=False
    )
```

```python
import heapq
import math

import jax
import jax.numpy as jnp
from jax import lax
from jax.experimental import pallas as pl
from jax.experimental.pallas import tpu as pltpu
from jax.sharding import PartitionSpec as P

MESH = pl.DeviceIdType.MESH
F32, BF16 = jnp.float32, jnp.bfloat16

HD, CH, R = 128, 64, 128
NX, NY, NZ = 4, 8, 8
TP, ROWS = 16, 32
TOK, HCOLS, WCOLS, KROWS = 256, 512, 256, 64
D = 8192
SPANS, HEADS = TOK // CH, HCOLS // HD
TOKZ, TOKD = TOK // NZ, TOK // TP
HALF = D // 2
G = 4
GC = HALF // G
GB = GC // WCOLS

SCORE_STEP = 1.5

PIECES = ((4,), (3, -3, 2, -2), (1, -1, 0))

PARTS = ((0, 208, 112), (208, 512, 352))

SCORE_AT = 36.0


def gather_plan():
    messages, needs = [], []

    def add(part, axis, sign, dx, dy, piece, need):
        lo, hi, mid = PARTS[part]
        lo, hi = ((lo, hi), (lo, mid), (mid, hi))[piece]
        messages.append((axis, sign, dx, dy, lo, hi))
        needs.append(need)
        return len(messages) - 1

    def ring(part, axis, size, other, need):
        got = {0: need}
        for sign in (1, -1):
            for step in range(size // 2):
                at = -sign * step
                last = step == size // 2 - 1
                piece = 0 if not last else (1 if sign == 1 else 2)
                dx, dy = (at, other) if axis == 0 else (other, at)
                bring = add(part, axis, sign, dx, dy, piece, got[at])
                key = size // 2 if last else at - sign
                got[key] = got.get(key, ()) + (bring,) if last else (bring,)
        return got

    for bx, need in ring(0, 0, NX, 0, ()).items():
        ring(0, 1, NY, bx, need)
    for by, need in ring(1, 1, NY, 0, ()).items():
        ring(1, 0, NX, by, need)

    count = len(messages)
    feeds = [[j for j in range(count) if i in needs[j]] for i in range(count)]
    depth = [0] * count
    for i in reversed(range(count)):
        depth[i] = max([1 + depth[j] for j in feeds[i]], default=0)
    rate, delay = 2 * WCOLS * 2 / 90e3, 1.5
    free = {}
    queue = []
    left = [len(n) for n in needs]

    def launch(i, now):
        axis, sign, _, _, lo, hi = messages[i]
        begin = max(now, free.get((axis, sign), 0.0))
        free[axis, sign] = begin + (hi - lo) * rate
        heapq.heappush(queue, (free[axis, sign] + delay, i))

    first = sorted((i for i in range(count) if not needs[i]), key=lambda i: (-depth[i], i))
    for i in first:
        launch(i, 0.0)
    steps = []
    while queue:
        now, i = heapq.heappop(queue)
        ready = []
        for j in feeds[i]:
            left[j] -= 1
            if left[j] == 0:
                ready.append(j)
        ready.sort(key=lambda j: (-depth[j], j))
        for j in ready:
            launch(j, now)
        steps.append((now, i, ready, not feeds[i]))
    return messages, first, steps


MESSAGES, FIRST, STEPS = gather_plan()


def wrap(axis, d):
    size = (NX, NY)[axis]
    return (d + size // 2 - 1) % size - (size // 2 - 1)


def came(i):
    axis, sign, dx, dy, _, _ = MESSAGES[i]
    return (wrap(0, dx - sign), wrap(1, dy)) if axis == 0 else (wrap(0, dx), wrap(1, dy - sign))


def arrival_order():
    when = {(0, 0): 0.0}
    for now, i, _, _ in STEPS:
        when[came(i)] = now
    return sorted(when, key=lambda at: (when[at], at))


ORDER = arrival_order()


def turns():
    passed = [(now, i, sends) for now, i, sends, last in STEPS if not last]
    chunk = {i: ORDER.index(came(i)) // (2 * GB) for _, i, _, _ in STEPS}
    signal = {i: n for n, (_, i, _) in enumerate(passed)}
    sizes, own = [], len(passed) + G
    for g in range(G):
        rest, alone, fits = [i for _, i, _, last in STEPS if last and chunk[i] == g], [], []
        while rest and not fits:
            total = sum(MESSAGES[i][5] - MESSAGES[i][4] for i in rest)
            fits = [k for k in range(1, ROWS) if total % (16 * k) == 0 and total // k <= HCOLS]
            if not fits:
                alone.append(rest.pop())
        signal.update({i: len(passed) + g for i in rest})
        signal.update({i: own + n for n, i in enumerate(alone)})
        own += len(alone)
        sizes.append(((fits[0], total // fits[0]) if rest else None, alone))
    return passed, signal, sizes, own


TURNS, SIGNAL, LATE, W_SEMS = turns()


def sum_plan():
    project_us, meet_us, small_us, link_us, delay_us = 2.4 / G, 1.3, 0.25, 5.8 / G, 1.6
    now, free = 0.0, 0.0
    ready = []
    order, left = [], list(range(G))
    while left or ready:
        able = sorted((-stage, g) for t, stage, g in ready if t <= now)
        if able:
            stage, g = -able[0][0], able[0][1]
            ready = [r for r in ready if r[1:] != (stage, g)]
            now += small_us
            order.append((1, g, 0) if stage == 0 else (2, g, stage) if stage < 4 else (3, g, 0))
            if stage < 4:
                free = max(now, free) + link_us * (0.5 if stage == 0 else 1.0)
                ready.append((free + delay_us, stage + 1, g))
        elif left:
            g = left.pop(0)
            order.append((0, g, 0))
            ready.append((now + project_us / 2 + meet_us, 0, g))
            now += project_us
        else:
            now = min(t for t, _, _ in ready)
    return order, now


SUMS, SUMS_US = sum_plan()


def kernel(
    idx_hbm, q_ref, k_ref, v_ref, res_ref, w_ref, out_ref,
    idx_ref, kbuf, vbuf, qbuf, rbuf, wbuf, attn, probs, xsend, xrecv, pown, first, last, shared, chains, ends,
    idx_sem, local_sem, kv_send, kv_recv, w_send, w_recv,
    x_send, x_recv, s_send, s_recv, c_send, c_recv, e_send, e_recv,
):
    row, tp = lax.axis_index("rows"), lax.axis_index("tp")
    x, y = row // NY, row % NY
    z, core = tp // 2, tp % 2
    sibling = z * 2 + (1 - core)

    def at_z(dz, dc=0):
        return ((z + dz) % NZ) * 2 + (core + dc) % 2

    def at_xy(axis, sign):
        if axis == 0:
            return ((x + sign) % NX) * NY + y
        return x * NY + (y + sign) % NY

    partners = [(row, sibling)]
    partners += [(row, at_z(dz, dc)) for dz in (4, 3, -3, 2, -2, 1, -1) for dc in (0, 1)]
    around = [(at_xy(axis, sign), tp) for axis in (0, 1) for sign in (1, -1)]

    barrier = pltpu.get_barrier_semaphore()
    for who in partners + around:
        pl.semaphore_signal(barrier, inc=1, device_id=who, device_id_type=MESH)

    own = (z, pl.ds(pl.multiple_of(core * KROWS, KROWS), KROWS))
    own_cols = pl.multiple_of(tp * HCOLS, HCOLS)

    fetch = pltpu.make_async_copy(idx_hbm, idx_ref, idx_sem)
    fetch.start()
    locals_ = [
        pltpu.make_async_copy(q_ref, qbuf, local_sem.at[0]),
        pltpu.make_async_copy(k_ref.at[:, pl.ds(own_cols, HCOLS)], kbuf.at[own], kv_recv.at[0]),
        pltpu.make_async_copy(v_ref.at[:, pl.ds(own_cols, HCOLS)], vbuf.at[own], kv_recv.at[1]),
        pltpu.make_async_copy(w_ref, wbuf.at[row], local_sem.at[3]),
        pltpu.make_async_copy(res_ref, rbuf, local_sem.at[4]),
    ]
    for copy in locals_:
        copy.start()
    pl.semaphore_wait(barrier, len(partners) + len(around))

    def owner(dx, dy):
        return ((x + dx) % NX) * NY + (y + dy) % NY

    def w_copy(i, arrived):
        axis, sign, dx, dy, lo, hi = MESSAGES[i]
        if arrived:
            dx, dy = (dx - sign, dy) if axis == 0 else (dx, dy - sign)
        slot = wbuf.at[owner(dx, dy), pl.ds(lo, hi - lo), :]
        mine = not arrived and dx == 0 and dy == 0
        return pltpu.make_async_remote_copy(
            src_ref=w_ref.at[pl.ds(lo, hi - lo), :] if mine else slot,
            dst_ref=slot,
            send_sem=w_send,
            recv_sem=w_recv.at[SIGNAL[i]],
            device_id=(at_xy(axis, sign), tp),
            device_id_type=MESH,
        )

    def send_kv(which):
        src, dst = ((k_ref, kbuf), (v_ref, vbuf))[which]
        for _, to in partners[1:] + partners[:1]:
            pltpu.make_async_remote_copy(
                src_ref=src.at[:, pl.ds(pl.multiple_of(to * HCOLS, HCOLS), HCOLS)],
                dst_ref=dst.at[own],
                send_sem=kv_send.at[which],
                recv_sem=kv_recv.at[which],
                device_id=(row, to),
                device_id_type=MESH,
            ).start()

    for i in FIRST:
        w_copy(i, False).start()
    send_kv(0)
    send_kv(1)
    def kv_wait(which):
        buf = (kbuf, vbuf)[which]
        pltpu.make_async_copy(buf, buf, kv_recv.at[which]).wait()
    def score(span):
        rows = pl.ds(span * CH, CH)
        keys = [kbuf[idx_ref[k, span]] for k in range(2)]
        for h in range(HEADS):
            query = qbuf[rows, h * HD:(h + 1) * HD]
            raw = jnp.concatenate(
                [
                    lax.dot_general(
                        query, block[:, h * HD:(h + 1) * HD], (((1,), (1,)), ((), ())),
                        preferred_element_type=F32,
                    )
                    for block in keys
                ],
                axis=1,
            ) * (1.0 / math.sqrt(HD))
            weights = jnp.exp(raw - jnp.max(raw, axis=1, keepdims=True))
            total = jnp.sum(weights, axis=1, keepdims=True)
            probs[rows, h * 2 * R:(h + 1) * 2 * R] = (weights / total).astype(BF16)

    def attend(span):
        rows = pl.ds(span * CH, CH)
        values = [vbuf[idx_ref[k, span]] for k in range(2)]
        for h in range(HEADS):
            value = jnp.concatenate([block[:, h * HD:(h + 1) * HD] for block in values], axis=0)
            out = jnp.dot(probs[rows, h * 2 * R:(h + 1) * 2 * R], value, preferred_element_type=F32)
            attn[rows, h * HD:(h + 1) * HD] = out.astype(BF16)

    locals_[0].wait()
    fetch.wait()
    turn = 0

    def pump(until):
        nonlocal turn
        while turn < len(TURNS) and TURNS[turn][0] < until:
            _, i, sends = TURNS[turn]
            w_copy(i, True).wait_recv()
            for j in sends:
                w_copy(j, False).start()
            turn += 1

    pump(SCORE_AT)
    kv_wait(0)
    for span in range(SPANS):
        score(span)
        pump(SCORE_AT + SCORE_STEP * (span + 1))
    pump(math.inf)
    kv_wait(1)
    for span in range(SPANS):
        attend(span)
    for copy in locals_[3:]:
        copy.wait()

    def block_of(side, g, j):
        (ax, ay), (bx, by) = (ORDER[(g * 2 + s) * GB + j] for s in range(2))
        return owner(ax + side * (bx - ax), ay + side * (by - ay))

    def arrived(g):
        shared_size, alone = LATE[g]
        for i in alone:
            w_copy(i, True).wait_recv()
        if shared_size:
            count, rows = shared_size
            part = wbuf.at[pl.ds(0, count), pl.ds(0, rows), :]
            pltpu.make_async_copy(part, part, w_recv.at[len(TURNS) + g]).wait()

    def tokens_of(dz, rows=TOKZ, base=0):
        return pl.ds(pl.multiple_of(((z + dz) % NZ) * TOKZ + base, rows), rows)

    def remote(src, dst, send, recv, to):
        return pltpu.make_async_remote_copy(
            src_ref=src, dst_ref=dst, send_sem=send, recv_sem=recv, device_id=(row, to), device_id_type=MESH
        )

    def chain(g, step, way):
        buf = chains.at[way, g]
        if step == 0:
            cols = pl.ds(way * (GC // 2), GC // 2)
            src, dst = first.at[g, :, cols], buf.at[0, :, cols]
        else:
            src, dst = buf.at[step - 1], buf.at[step]
        return remote(src, dst, c_send, c_recv.at[way, g, step], at_z(1 - 2 * way))

    def last_hop(g, way, dc):
        rows = pl.ds(pl.multiple_of(((core + dc) % 2) * TOKD, TOKD), TOKD)
        return remote(
            chains.at[way, g, 2, rows], ends.at[g, way, dc],
            e_send, e_recv.at[g], at_z(1 - 2 * way, dc),
        )

    def exchange(g, piece):
        for dz in PIECES[piece]:
            rows = tokens_of(dz)
            remote(xsend.at[g, rows], xrecv.at[g, rows], x_send, x_recv.at[g, piece], sibling).start()

    def met(g, piece):
        part = xrecv.at[g, pl.ds(0, len(PIECES[piece]) * TOKZ)]
        pltpu.make_async_copy(part, part, x_recv.at[g, piece]).wait()

    def both(g, rows, cols=slice(None)):
        return pown[g, rows, cols] + xrecv[g, rows, cols].astype(F32)

    def share(g):
        return remote(last.at[g], shared.at[g], s_send, s_recv.at[g], sibling)

    def project(g):
        arrived(g)
        for other in (True, False):
            side = 1 - core if other else core
            for j in range(GB):
                part = jnp.dot(attn[...], wbuf[block_of(side, g, j)], preferred_element_type=F32)
                cols = slice(j * WCOLS, (j + 1) * WCOLS)
                if other:
                    xsend[g, :, cols] = part.astype(BF16)
                else:
                    pown[g, :, cols] = part
            if other:
                exchange(g, 0)
        exchange(g, 1)

    def start(g):
        met(g, 0)
        first[g] = both(g, tokens_of(4)).astype(BF16)
        for way in range(2):
            chain(g, 0, way).start()
        exchange(g, 2)

    def relay(g, step):
        if step != 2:
            met(g, 1 if step == 1 else 2)
        for way in range(2):
            chain(g, step - 1, way).wait_recv()
            buf = chains.at[way, g, step - 1]
            tokens = tokens_of((1 - 2 * way) * (4 - step))
            if step == 1:
                cut = GC // 2
                got, rest = slice(way * cut, (way + 1) * cut), slice((1 - way) * cut, (2 - way) * cut)
                buf[:, got] = (buf[:, got].astype(F32) + both(g, tokens, got)).astype(BF16)
                buf[:, rest] = both(g, tokens, rest).astype(BF16)
            else:
                buf[...] = (buf[...].astype(F32) + both(g, tokens)).astype(BF16)
            if step < 3:
                chain(g, step, way).start()
            else:
                for dc in (1, 0):
                    last_hop(g, way, dc).start()
        if step == 3:
            last[g] = both(g, tokens_of(0, TOKD, (1 - core) * TOKD)).astype(BF16)
            share(g).start()

    def finish(g):
        share(g).wait_recv()
        pltpu.make_async_copy(ends.at[g], ends.at[g], e_recv.at[g]).wait()
        mine = tokens_of(0, TOKD, core * TOKD)
        for dc in range(2):
            side = core if dc == 0 else 1 - core
            for j in range(GB):
                at = pl.ds(pl.multiple_of(block_of(side, g, j) * WCOLS, WCOLS), WCOLS)
                cols = slice(j * WCOLS, (j + 1) * WCOLS)
                here = both(g, mine, cols) if dc == 0 else shared[g, :, cols].astype(F32)
                out_ref[:, at] = (
                    rbuf[:, at].astype(F32)
                    + here
                    + ends[g, 0, dc, :, cols].astype(F32)
                    + ends[g, 1, dc, :, cols].astype(F32)
                ).astype(BF16)

    for what, g, step in SUMS:
        if what == 0:
            project(g)
        elif what == 1:
            start(g)
        elif what == 2:
            relay(g, step)
        else:
            finish(g)
    sent = wbuf.at[pl.ds(0, 2 * G * 5 * GB * TOKZ // 2 // HCOLS)]
    for part, sem in ((xsend, x_send), (shared, s_send), (ends, e_send), (sent, c_send)):
        pltpu.make_async_copy(part, part, sem).wait()
    waitbuf = wbuf.at[pl.ds(0, TP - 1), pl.ds(0, KROWS * HCOLS // WCOLS), :]
    for which in range(2):
        pltpu.make_async_copy(waitbuf, waitbuf, kv_send.at[which]).wait()
    rest = wbuf.at[pl.ds(0, ROWS - 1)]
    pltpu.make_async_copy(rest, rest, w_send).wait()


def solution(mesh):
    def shards(queries, nbr_keys, nbr_values, nbr_index, residual, out_weight):
        hbm = pl.BlockSpec(memory_space=pl.ANY)
        dma = pltpu.SemaphoreType.DMA
        return pl.pallas_call(
            kernel,
            out_shape=jax.ShapeDtypeStruct((TOKD, D), BF16),
            in_specs=[hbm] * 6,
            out_specs=pl.BlockSpec(memory_space=pltpu.VMEM),
            scratch_shapes=[
                pltpu.SMEM((2, SPANS), jnp.int32),
                pltpu.VMEM((NZ, R, HCOLS), BF16),
                pltpu.VMEM((NZ, R, HCOLS), BF16),
                pltpu.VMEM((TOK, HCOLS), BF16),
                pltpu.VMEM((TOKD, D), BF16),
                pltpu.VMEM((ROWS, HCOLS, WCOLS), BF16),
                pltpu.VMEM((TOK, HCOLS), BF16),
                pltpu.VMEM((TOK, HEADS * 2 * R), BF16),
                pltpu.VMEM((G, TOK, GC), BF16),
                pltpu.VMEM((G, TOK, GC), BF16),
                pltpu.VMEM((G, TOK, GC), F32),
                pltpu.VMEM((G, TOKZ, GC), BF16),
                pltpu.VMEM((G, TOKD, GC), BF16),
                pltpu.VMEM((G, TOKD, GC), BF16),
                pltpu.VMEM((2, G, 3, TOKZ, GC), BF16),
                pltpu.VMEM((G, 2, 2, TOKD, GC), BF16),
                dma, dma((5,)), dma((2,)), dma((2,)), dma, dma((W_SEMS,)),
                dma, dma((G, len(PIECES))), dma, dma((G,)), dma, dma((2, G, 3)), dma, dma((G,)),
            ],
            compiler_params=pltpu.CompilerParams(
                collective_id=0, has_side_effects=True, vmem_limit_bytes=56 * 1024 * 1024
            ),
            cost_estimate=pl.CostEstimate(flops=2_400_000_000, bytes_accessed=12_000_000, transcendentals=262144),
        )(nbr_index.T, queries, nbr_keys, nbr_values, residual, out_weight)

    placed = (
        P("rows", "tp"),
        P(("rows", "tp"), None),
        P(("rows", "tp"), None),
        P("rows", None),
        P(("rows", "tp"), None),
        P("tp", "rows"),
    )
    return jax.shard_map(
        shards, mesh=mesh, in_specs=placed, out_specs=P(("rows", "tp"), None), check_vma=False
    )
```
